512 devices in a mesh: tenant: 8 (over z), expert: 64 (over y, x, core).
Axes of the slice: x: 4, y: 8, z: 8, core: 2. Of those that a mesh axis runs over, the one named last changes fastest.
Arguments:
- d_out: bfloat16 [65536, 4096], P(('tenant', 'expert')), may hold values from -6 to 6
- normed: bfloat16 [65536, 4096], P(('tenant', 'expert')), may hold values from -6 to 6
- rstd: float32 [65536], P(('tenant', 'expert')), may hold values from 0.3 to 3
- gain: float32 [4096], replicated, may hold values from 0.1 to 1.9
- expert_grads: bfloat16 [8, 64, 64, 4, 4096], P('tenant', 'expert'), may hold values from -6 to 6
- expert_ids: int32 [65536, 1], P(('tenant', 'expert')), may hold values from 0 to 63; in each aligned block of 128 rows (0 to 127, 128 to 255, ...) at most 4 rows name the same one
- low_rank: bfloat16 [65536, 16], P(('tenant', 'expert')), may hold values from -6 to 6
- lengths: int32 [4096], P(('tenant', 'expert')), may hold values from 1 to 16
- tenant_ids: int32 [4096], P(('tenant', 'expert')), may hold values from 0 to 31, as said below
- adapters: bfloat16 [32, 16, 4096], P('tenant'), may hold values from -1.5 to 1.5
Outputs:
- grad_b: float32 [32, 65536], P('tenant', 'expert')
- low_rank_grad: bfloat16 [65536, 16], P(('tenant', 'expert'))
The draws below stay inside these ranges and needn't reach their ends.
Inputs may be any that keep to these rules, and one draw needn't show every extreme that they name: `expert_ids`: among one device's 128 token slots no expert is named more than 4 times, a bound that some block reaches. `tenant_ids`: the j-th block (from 0) of every device belongs to a tenant t with t // 4 == j.
All inputs are finite; a program needn't handle non-finite values.
Results may differ from the reference program's by a relative error of at most 0.0049.
Values may be sent and summed in bfloat16 or wider, within the bound.
No kernel may reach another device: no remote copies, remote signals or barrier semaphores. Data moves between devices by JAX's collectives and lax.ppermute only.
A program may use at most 128 MiB of HBM per device.

```python
import math
import jax
import jax.numpy as jnp
import numpy as np
from jax import lax

D = 4096
RANK = 16
TOK_DEV = 128
TEN_DEV = 4
TOPK = 1
EXPERTS = 64
MOST = 4
BLK = 16
TENANTS = 32
TOKENS = 65536
BLOCKS = 4096
N_TENANT = 8
N_EXPERT = 64


def draw_tenant_ids(key, part):
    key = jax.random.fold_in(key, 7)
    block_total = TOKENS // BLK
    owner_count = TENANTS // TEN_DEV
    local_ids = jax.random.randint(key, (block_total,), 0, TEN_DEV)
    owner_of = jnp.arange(block_total, dtype=jnp.int32) % owner_count
    return (owner_of * TEN_DEV + local_ids).astype(jnp.int32)


def touch_ends(drawn, own_key, least, largest):
    longest = drawn.shape.index(max(drawn.shape))
    spots = []
    for shift in (0, 1):
        where = [jax.random.randint(jax.random.fold_in(own_key, axis), (), 0, length) for axis, length in enumerate(drawn.shape)]
        where[longest] = (where[longest] + shift) % drawn.shape[longest]
        spots.append(tuple(where))
    return drawn.at[spots[0]].set(least).at[spots[1]].set(largest)


def block_scale(rng, dims, pieces, low, high):
    def one(dim, shards_of):
        heights = jax.random.uniform(jax.random.fold_in(jax.random.fold_in(rng, 6), dim), (shards_of,), jnp.float32, low / len(pieces), high / len(pieces))
        return jnp.repeat(jnp.exp(heights), dims[dim] // shards_of).reshape((-1,) + (1,) * (len(dims) - dim - 1))

    loudness = one(*pieces[0])
    for cut in pieces[1:]:
        loudness = loudness * one(*cut)
    return loudness


def routed_block(key, own, number, rows, count, top, reach, slope):
    order = jax.random.permutation(key, count)
    packed, usual = portions_of(count, rows * top, reach, slope, True), portions_of(count, rows * top, reach, slope, False)
    places = jnp.arange(count)

    def named(sizes, turn):
        used = int((sizes > 0).sum())
        fixed = max(1, used // 4)
        passed = fixed + (places - fixed + turn * (used - fixed)) % max(1, count - fixed)
        return jnp.zeros((count,), jnp.int32).at[order[jnp.where(places < fixed, places, passed)]].set(jnp.asarray(sizes, jnp.int32))

    sizes = jnp.where(number % 4 == 0, named(packed, number // 4), named(usual, number - number // 4 - 1))
    mixed = jax.random.permutation(jax.random.fold_in(own, 3), count)
    source_of, receiver = mixed[0:count // 2 * 2:2], mixed[1:count // 2 * 2:2]
    room = jnp.minimum(sizes[source_of] - 1, reach - sizes[receiver]) // 2
    room = jnp.where((source_of == order[0]) | (receiver == order[0]) | (sizes[receiver] == 0), 0, jnp.maximum(room, 0))
    passed = jax.random.randint(jax.random.fold_in(own, 4), (count // 2,), 0, 1 << 20) % (room + 1)
    sizes = sizes.at[source_of].add(-passed).at[receiver].add(passed)
    labels = jnp.searchsorted(jnp.cumsum(sizes), jnp.arange(rows * top), side="right").astype(jnp.int32)
    table = labels.reshape(top, rows).T
    table = table[jax.random.permutation(jax.random.fold_in(own, 1), rows)]
    turn = jax.random.randint(jax.random.fold_in(own, 2), (rows, 1), 0, top)
    return jnp.take_along_axis(table, (jnp.arange(top)[None, :] + turn) % top, axis=1)


def portions_of(amount, total, reach, slope, full):
    loads = [(1 << 20) // math.isqrt(grade ** slope) + 1 for grade in range(1, amount + 1)]
    largest = reach if full else min(reach, max(-(-total // amount), total * loads[0] // sum(loads)))
    least = 1 if total - largest >= amount - 1 else 0
    given, surplus = [largest] + [least] * (amount - 1), total - largest - least * (amount - 1)
    while surplus > 0:
        movable = [i for i in range(1, amount) if given[i] < largest] or [i for i in range(1, amount) if given[i] < reach]
        mass, budget = sum([loads[i] for i in movable]), surplus
        for i in movable:
            more = min(reach - given[i], max(1, budget * loads[i] // mass), surplus)
            given[i] = given[i] + more
            surplus = surplus - more
    return np.array(given)


def centred(key, dims, scale, bound, pieces=(), held_as=jnp.bfloat16):
    array = scale * jax.random.normal(key, dims, jnp.float32)
    if pieces:
        array = array * block_scale(key, dims, pieces, -0.22, 0.18)
    return jnp.clip(array, -bound, bound).astype(held_as)


def setup_inputs(seed: int = 0) -> dict:
    keys = jax.random.split(jax.random.key(seed), 11)
    d_out = centred(keys[0], (TOKENS, D), 1.0, 6.0, ((0, 512),))
    normed = centred(keys[1], (TOKENS, D), 1.0, 6.0, ((0, 512),))
    rstd = jnp.clip(jnp.exp(math.log(3.0) - 2.3025851 * jax.random.uniform(keys[2], (TOKENS,), jnp.float32) ** block_scale(keys[2], (TOKENS,), ((0, 512),), -0.2, 0.2)), 0.3, 3.0)
    gain = jnp.clip(1.0 + 0.18 * jax.random.normal(keys[3], (D,), jnp.float32), 0.1, 1.9)
    expert_grads = centred(keys[4], (N_TENANT, N_EXPERT, N_EXPERT, MOST, D), 1.0, 6.0, ((0, 8), (1, 64)))
    expert_ids_keys = jax.random.split(jax.random.fold_in(keys[5], 1), TOKENS // TOK_DEV)
    expert_ids_turns = jax.random.permutation(jax.random.fold_in(keys[5], 3), TOKENS // TOK_DEV)
    expert_ids = jax.vmap(lambda own, number: routed_block(jax.random.fold_in(keys[5], 2), own, number, TOK_DEV, EXPERTS, TOPK, MOST, 2))(expert_ids_keys, expert_ids_turns).reshape((TOKENS, TOPK))
    low_rank = centred(keys[6], (TOKENS, RANK), 1.0, 6.0, ((0, 512),))
    lengths = touch_ends(jax.random.randint(keys[7], (BLOCKS,), 1, BLK + 1), jax.random.fold_in(keys[7], 1), 1, BLK).astype(jnp.int32)
    tenant_ids = draw_tenant_ids(jax.random.fold_in(keys[10], 71), 0)
    adapters = centred(keys[9], (TENANTS, RANK, D), RANK ** -0.5, 1.5, ((0, 8),))
    return {"d_out": d_out, "normed": normed, "rstd": rstd, "gain": gain, "expert_grads": expert_grads, "expert_ids": expert_ids, "low_rank": low_rank, "lengths": lengths, "tenant_ids": tenant_ids, "adapters": adapters}


def reference(d_out, normed, rstd, gain, expert_grads, expert_ids, low_rank, lengths, tenant_ids, adapters):
    col_count = N_EXPERT
    row_count = N_TENANT
    b_flat = adapters.reshape(TENANTS * RANK, D)
    row_items = (
        d_out.reshape(row_count, col_count, TOK_DEV, D),
        normed.reshape(row_count, col_count, TOK_DEV, D),
        rstd.reshape(row_count, col_count, TOK_DEV),
        expert_grads,
        expert_ids.reshape(row_count, col_count, TOK_DEV),
        low_rank.reshape(row_count, col_count, TOK_DEV, RANK),
        lengths.reshape(row_count, col_count, N_TENANT),
        tenant_ids.reshape(row_count, col_count, N_TENANT),
    )

    def row_step(summed, items):
        out_rows, normed_rows, scale_rows, row_grads, route_ids, low_rows, length_rows, tenant_rows = items
        onehot = (route_ids[..., None] == jnp.arange(EXPERTS, dtype=jnp.int32)).astype(jnp.int32)
        before = jnp.cumsum(onehot, axis=1) - onehot
        slot_ids = jnp.sum(before * onehot, axis=-1).astype(jnp.int32)
        source_cols = jnp.arange(col_count, dtype=jnp.int32)[:, None]
        moe_grad = row_grads[route_ids, source_cols, slot_ids]
        weighted = gain * moe_grad.astype(jnp.float32)
        normed_f = normed_rows.astype(jnp.float32)
        centre = jnp.mean(weighted * normed_f, axis=-1, keepdims=True)
        norm_grad = scale_rows[..., None] * (weighted - normed_f * centre)
        position = jnp.arange(TOK_DEV, dtype=jnp.int32)
        block_of = position // BLK
        within = position % BLK
        is_valid = within[None, :] < length_rows[:, block_of]
        total = out_rows.astype(jnp.float32) + norm_grad
        cotangent = jnp.where(is_valid[..., None], total, 0.0).astype(jnp.bfloat16)
        token_tenant = tenant_rows[:, block_of]
        chosen = (token_tenant[..., None] == jnp.arange(TENANTS, dtype=jnp.int32)).astype(jnp.bfloat16)
        spread = (chosen[..., None] * low_rows[:, :, None, :]).reshape(col_count * TOK_DEV, TENANTS * RANK)
        cot_flat = cotangent.reshape(col_count * TOK_DEV, D)
        summed = summed + jnp.dot(spread.T, cot_flat, preferred_element_type=jnp.float32)
        projected = jnp.dot(cot_flat, b_flat.T, preferred_element_type=jnp.float32)
        chosen_f = chosen.astype(jnp.float32).reshape(col_count * TOK_DEV, TENANTS, 1)
        low_grad = jnp.sum(projected.reshape(col_count * TOK_DEV, TENANTS, RANK) * chosen_f, axis=1)
        return summed, low_grad.astype(jnp.bfloat16)

    start = jnp.zeros((TENANTS * RANK, D), jnp.float32)
    summed, low_grads = lax.scan(row_step, start, row_items)
    grad_b = summed.reshape(TENANTS, RANK * D)
    low_rank_grad = low_grads.reshape(TOKENS, RANK)
    return (grad_b, low_rank_grad)
```

```python
import functools

import jax
import jax.numpy as jnp
from jax import lax
from jax.experimental import pallas as pl
from jax.experimental.pallas import tpu as pltpu
from jax.sharding import Mesh
from jax.sharding import PartitionSpec as P

ALL = ("z", "y", "x", "c")
CHUNK = 512
PAD = 128
BF = jnp.bfloat16
F32 = jnp.float32


def exchange(array, axes):
    return lax.all_to_all(array, axes, split_axis=0, concat_axis=0, tiled=True)


def cotangent_kernel(
    recv_ref, pick_ref, normed_ref, out_grad_ref, gain_ref, rstd_ref, valid_ref, spread_ref, marks_ref,
    terms_ref, cot_ref, moe_ref
):
    width = normed_ref.shape[1]
    slots = recv_ref.shape[0] * recv_ref.shape[1]
    pairs = terms_ref.shape[0]
    pick = pick_ref[...]
    total = None
    for start in range(0, width, CHUNK):
        cols = slice(start, start + CHUNK)
        rows = recv_ref[:, :, cols].reshape(slots, CHUNK)
        moe = jnp.dot(pick, rows, preferred_element_type=F32)
        moe_ref[:, cols] = moe.astype(BF)
        part = gain_ref[:, cols] * moe * normed_ref[:, cols].astype(F32)
        total = part if total is None else total + part
    centre = jnp.sum(total, axis=1, keepdims=True) * (1.0 / width)
    rstd = rstd_ref[...]
    keep = valid_ref[...] > 0.0
    spread = spread_ref[...]
    for start in range(0, width, CHUNK):
        cols = slice(start, start + CHUNK)
        weighted = gain_ref[:, cols] * moe_ref[:, cols].astype(F32)
        norm_grad = rstd * (weighted - normed_ref[:, cols].astype(F32) * centre)
        added = out_grad_ref[:, cols].astype(F32) + norm_grad
        cot = jnp.where(keep, added, 0.0).astype(BF)
        cot_ref[:, cols] = cot
        terms = jnp.dot(spread, cot, preferred_element_type=F32).astype(BF)
        terms_ref[:, :, cols] = terms.reshape(pairs, 2, CHUNK)
    terms_ref[:, :, width:] = marks_ref[...]


def sum_kernel(terms_ref, sums_ref):
    sources, _, padded = terms_ref.shape
    width = padded - PAD
    quarter = sums_ref.shape[2]
    tenants = sums_ref.shape[1]
    marks = terms_ref[:, :, width:].reshape(2 * sources, PAD).astype(F32)
    row = lax.broadcasted_iota(jnp.int32, (2 * sources, PAD), 0)
    lane = lax.broadcasted_iota(jnp.int32, (2 * sources, PAD), 1)
    wanted = (lane % tenants).astype(F32)
    hit = (marks == wanted) & (row % 2 == lane // tenants)
    chosen = jnp.where(hit, 1.0, 0.0).astype(BF).T[: 2 * tenants]
    for part in range(width // quarter):
        cols = slice(part * quarter, (part + 1) * quarter)
        rows = terms_ref[:, :, cols].reshape(2 * sources, quarter)
        sums = jnp.dot(chosen, rows, preferred_element_type=F32)
        sums_ref[part] = sums[:tenants]
        sums_ref[width // quarter + part] = sums[tenants:]


def per_device(
    d_out, normed, rstd, gain, expert_grads, expert_ids, low_rank, lengths, tenant_ids, adapters
):
    tok_count, model_width = d_out.shape
    expert_count, slot_count = expert_grads.shape[2], expert_grads.shape[3]
    tenant_count = lax.axis_size("z")
    block_size = tok_count // tenant_count
    ten_dev, rank_size = adapters.shape[0], adapters.shape[1]
    y_count = lax.axis_size("y")

    returned = exchange(expert_grads[0, 0], ("y", "x", "c"))
    all_adapters = lax.all_gather(
        adapters.reshape(ten_dev * rank_size, model_width), "z", axis=0, tiled=True
    )

    routes = expert_ids[:, 0]
    onehot = (routes[:, None] == jnp.arange(expert_count, dtype=jnp.int32)[None, :]).astype(F32)
    position = jnp.arange(tok_count, dtype=jnp.int32)
    earlier = (position[:, None] > position[None, :]).astype(F32)
    before = jnp.dot(earlier, onehot, preferred_element_type=F32)
    slot_ids = jnp.sum(before * onehot, axis=1).astype(jnp.int32)
    flat_slot = routes * slot_count + slot_ids
    pick = (
        flat_slot[:, None] == jnp.arange(expert_count * slot_count, dtype=jnp.int32)[None, :]
    ).astype(BF)
    valid = (
        jnp.arange(block_size, dtype=jnp.int32)[None, :] < lengths[:, None]
    ).astype(F32).reshape(tok_count, 1)
    block_of = position // block_size
    low_t = jnp.tile(low_rank.T, (tenant_count, 1))
    spread = jnp.where(block_of[:, None] == block_of[None, :], low_t, jnp.zeros((), BF))
    local_ids = tenant_ids - jnp.arange(tenant_count, dtype=jnp.int32) * ten_dev
    marks = jnp.broadcast_to(
        local_ids.astype(BF)[:, None, None, None], (tenant_count, y_count, 2, PAD)
    ).reshape(tenant_count * y_count, 2, PAD)

    terms, cotangent = pl.pallas_call(
        cotangent_kernel,
        out_shape=(
            jax.ShapeDtypeStruct((tenant_count * y_count, 2, model_width + PAD), BF),
            jax.ShapeDtypeStruct((tok_count, model_width), BF),
        ),
        in_specs=[pl.BlockSpec(memory_space=pltpu.VMEM)] * 9,
        out_specs=(pl.BlockSpec(memory_space=pltpu.VMEM),) * 2,
        scratch_shapes=[pltpu.VMEM((tok_count, model_width), BF)],
        compiler_params=pltpu.CompilerParams(vmem_limit_bytes=40 * 1024 * 1024),
        name="cotangent",
    )(returned, pick, normed, d_out, gain[None, :], rstd[:, None], valid, spread, marks)

    arrived = exchange(terms, ("z", "y"))

    projected = lax.dot_general(
        cotangent, all_adapters, (((1,), (1,)), ((), ())), preferred_element_type=F32
    )
    chosen = jnp.repeat(
        tenant_ids[:, None] == jnp.arange(tenant_count * ten_dev, dtype=jnp.int32)[None, :],
        block_size,
        axis=0,
    )
    low_rank_grad = jnp.sum(
        jnp.where(
            chosen[:, :, None],
            projected.reshape(tok_count, tenant_count * ten_dev, rank_size),
            0.0,
        ),
        axis=1,
    ).astype(BF)

    column_parts = lax.axis_size("x") * lax.axis_size("c")
    sums = pl.pallas_call(
        sum_kernel,
        out_shape=jax.ShapeDtypeStruct((column_parts, ten_dev, 2 * model_width // column_parts), F32),
        in_specs=[pl.BlockSpec(memory_space=pltpu.VMEM)],
        out_specs=pl.BlockSpec(memory_space=pltpu.VMEM),
        compiler_params=pltpu.CompilerParams(vmem_limit_bytes=40 * 1024 * 1024),
        name="tenant_sums",
    )(arrived)
    grad_b = jnp.sum(exchange(sums, ("x", "c")), axis=0)
    return (grad_b, low_rank_grad)


def solution(mesh):
    fine = Mesh(mesh.devices.reshape(8, 8, 4, 2), ALL)
    expert = ("y", "x", "c")
    placed = (
        P(ALL, None),
        P(ALL, None),
        P(ALL),
        P(),
        P("z", expert, None, None, None),
        P(ALL, None),
        P(ALL, None),
        P(ALL),
        P(ALL),
        P("z", None, None),
    )
    return jax.shard_map(
        per_device,
        mesh=fine,
        in_specs=placed,
        out_specs=(P("z", expert), P(ALL, None)),
        check_vma=False,
    )
```

```python
import jax
import jax.numpy as jnp
import numpy as np
from jax import lax
from jax.experimental import pallas as pl
from jax.experimental.pallas import tpu as pltpu
from jax.sharding import Mesh
from jax.sharding import PartitionSpec as P

ALL = ("z", "y", "x", "c")
CHUNK = 512
PAD = 128
BF = jnp.bfloat16
F32 = jnp.float32
STEPS = ((0, 4), (1, 7), (2, 6), (3, 5))


def exchange(array, axes):
    return lax.all_to_all(array, axes, split_axis=0, concat_axis=0, tiled=True)


def cotangent_kernel(
    ids_ref, place_ref, recv_ref, pick_ref, gain_ref, rstd_ref, spread_ref, normed_hbm, out_grad_hbm, *rest
):
    terms_hbm, *sent_hbm = rest[-12:-7]
    normed_ref, out_grad_ref, moe_ref, cot_ref, terms_ref, in_sems, out_sems = rest[-7:]
    fetch_normed = pltpu.make_async_copy(normed_hbm, normed_ref, in_sems.at[0])
    fetch_out = pltpu.make_async_copy(out_grad_hbm, out_grad_ref, in_sems.at[1])
    fetch_normed.start()
    fetch_out.start()
    tokens, width = normed_ref.shape
    slots = recv_ref.shape[0] * recv_ref.shape[1]
    pairs = terms_ref.shape[0]
    blocks = ids_ref.shape[0]
    block_size = tokens // blocks
    held = sent_hbm[0].shape[0]
    pick = pick_ref[...]
    for start in range(0, width, CHUNK):
        cols = slice(start, start + CHUNK)
        rows = recv_ref[:, :, cols].reshape(slots, CHUNK)
        moe_ref[:, cols] = jnp.dot(pick, rows, preferred_element_type=F32).astype(BF)
    for block in range(blocks):
        mark = ids_ref[block].astype(F32).astype(BF)
        here = slice(block * pairs // blocks, (block + 1) * pairs // blocks)
        terms_ref[here, :, width:] = jnp.full((pairs // blocks, 2, PAD), mark)
        rows = slice(block * block_size, (block + 1) * block_size)
        cot_ref[rows, width:] = jnp.full((block_size, PAD), mark)
    fetch_normed.wait()
    total = None
    for start in range(0, width, CHUNK):
        cols = slice(start, start + CHUNK)
        part = gain_ref[:, cols] * moe_ref[:, cols].astype(F32) * normed_ref[:, cols].astype(F32)
        total = part if total is None else total + part
    centre = jnp.sum(total, axis=1, keepdims=True) * (1.0 / width)
    rstd = rstd_ref[...]
    keep = rstd > 0.0
    spread = spread_ref[...]
    fetch_out.wait()
    stores = []
    for start in range(0, width, CHUNK):
        cols = slice(start, start + CHUNK)
        weighted = gain_ref[:, cols] * moe_ref[:, cols].astype(F32)
        norm_grad = rstd * (weighted - normed_ref[:, cols].astype(F32) * centre)
        cot = jnp.where(keep, out_grad_ref[:, cols].astype(F32) + norm_grad, 0.0).astype(BF)
        cot_ref[:, cols] = cot
        terms = jnp.dot(spread, cot, preferred_element_type=F32).astype(BF)
        terms_ref[:, :, cols] = terms.reshape(pairs, 2, CHUNK)
        last = start + CHUNK == width
        done = pl.ds(start, CHUNK + PAD if last else CHUNK)
        store = pltpu.make_async_copy(
            terms_ref.at[:, :, done], terms_hbm.at[:, :, done], out_sems.at[blocks + len(stores)]
        )
        store.start()
        stores.append(store)

    def for_blocks(act):
        for block in range(blocks):
            place = place_ref[block]
            rows = pl.ds(block * block_size, block_size)
            for where, target in enumerate(sent_hbm):

                @pl.when(place // held == where)
                def _():
                    act(
                        pltpu.make_async_copy(
                            cot_ref.at[rows, :], target.at[place % held], out_sems.at[block]
                        )
                    )

    for_blocks(lambda copy: copy.start())
    for store in stores:
        store.wait()
    for_blocks(lambda copy: copy.wait())


def low_rank_kernel(*refs):
    sharers = len(STEPS)
    cots, shards, outs = refs[:sharers], refs[sharers:-sharers], refs[-sharers:]
    block_size = cots[0].shape[1]
    width = cots[0].shape[2] - PAD
    rank = outs[0].shape[2]
    tenants = shards[0].shape[0] // rank
    for turn in range(len(shards)):
        rows = jnp.concatenate([cot[turn, :, :width] for cot in cots], axis=0)
        marks = jnp.concatenate([cot[turn, :, width:] for cot in cots], axis=0).astype(F32)
        projected = lax.dot_general(
            rows, shards[turn][...], (((1,), (1,)), ((), ())), preferred_element_type=F32
        )
        lane = lax.broadcasted_iota(jnp.int32, projected.shape, 1)
        hit = (lane // rank).astype(F32) == marks[:, : tenants * rank]
        chosen = jnp.where(hit, projected, 0.0)
        total = chosen[:, :rank]
        for tenant in range(1, tenants):
            total = total + chosen[:, tenant * rank : (tenant + 1) * rank]
        for index, out in enumerate(outs):
            out[turn] = total[index * block_size : (index + 1) * block_size].astype(BF)


def sum_kernel(terms_ref, _, sums_ref):
    sources, _, padded = terms_ref.shape
    width = padded - PAD
    quarter = sums_ref.shape[2]
    tenants = sums_ref.shape[1]
    marks = terms_ref[:, :, width:].reshape(2 * sources, PAD).astype(F32)
    row = lax.broadcasted_iota(jnp.int32, (2 * sources, PAD), 0)
    lane = lax.broadcasted_iota(jnp.int32, (2 * sources, PAD), 1)
    wanted = (lane % tenants).astype(F32)
    hit = (marks == wanted) & (row % 2 == lane // tenants)
    chosen = jnp.where(hit, 1.0, 0.0).astype(BF).T[: 2 * tenants]
    for part in range(width // quarter):
        cols = slice(part * quarter, (part + 1) * quarter)
        rows = terms_ref[:, :, cols].reshape(2 * sources, quarter)
        sums = jnp.dot(chosen, rows, preferred_element_type=F32)
        sums_ref[part] = sums[:tenants]
        sums_ref[width // quarter + part] = sums[tenants:]


def per_device(
    d_out, normed, rstd, gain, expert_grads, expert_ids, low_rank, lengths, tenant_ids, adapters
):
    tok_count, model_width = d_out.shape
    expert_count, slot_count = expert_grads.shape[2], expert_grads.shape[3]
    tenant_count = lax.axis_size("z")
    block_size = tok_count // tenant_count
    ten_dev, rank_size = adapters.shape[0], adapters.shape[1]
    y_count = lax.axis_size("y")

    returned = exchange(expert_grads[0, 0], ("y", "x", "c"))

    owner = lax.axis_index("z")
    kind = lax.axis_index("x") % 2 * 2 + lax.axis_index("c")
    x_count, c_count = lax.axis_size("x"), lax.axis_size("c")
    sharers, held = len(STEPS), len(STEPS[0])
    shard = adapters.reshape(ten_dev * rank_size, model_width)
    shards = [
        lax.ppermute(
            shard,
            ("z", "x", "c"),
            [
                (
                    ((z + STEPS[x % 2 * 2 + c][turn]) % tenant_count * x_count + x) * c_count + c,
                    (z * x_count + x) * c_count + c,
                )
                for z in range(tenant_count)
                for x in range(x_count)
                for c in range(c_count)
            ],
        )
        for turn in range(held)
    ]
    local_ids = tenant_ids - jnp.arange(tenant_count, dtype=jnp.int32) * ten_dev
    codes = np.zeros(tenant_count, np.int32)
    for index, (first, second) in enumerate(STEPS):
        codes[first], codes[second] = index * held, index * held + 1
    block_index = jnp.arange(tenant_count, dtype=jnp.int32)
    step = (block_index - owner) % tenant_count
    code = jnp.sum(jnp.where(step[:, None] == block_index[None, :], codes[None, :], 0), axis=1)
    place = (code ^ (kind * held)).astype(jnp.int32)

    routes = expert_ids[:, 0]
    onehot = (routes[:, None] == jnp.arange(expert_count, dtype=jnp.int32)[None, :]).astype(F32)
    position = jnp.arange(tok_count, dtype=jnp.int32)
    earlier = (position[:, None] > position[None, :]).astype(F32)
    before = jnp.dot(earlier, onehot, preferred_element_type=F32)
    slot_ids = jnp.sum(before * onehot, axis=1).astype(jnp.int32)
    flat_slot = routes * slot_count + slot_ids
    pick = (
        flat_slot[:, None] == jnp.arange(expert_count * slot_count, dtype=jnp.int32)[None, :]
    ).astype(BF)
    valid = (
        jnp.arange(block_size, dtype=jnp.int32)[None, :] < lengths[:, None]
    ).reshape(tok_count, 1)
    zero = jnp.zeros((), BF)
    rstd_kept = jnp.where(valid, rstd[:, None], 0.0)
    block_of = position // block_size
    low_t = jnp.tile(low_rank.T, (tenant_count, 1))
    spread = jnp.where(block_of[:, None] == block_of[None, :], low_t, zero)

    vmem = pl.BlockSpec(memory_space=pltpu.VMEM)
    smem = pl.BlockSpec(memory_space=pltpu.SMEM)
    grant = pltpu.CompilerParams(vmem_limit_bytes=24 * 1024 * 1024)
    hbm = pl.BlockSpec(memory_space=pl.ANY)
    terms_shape = (tenant_count * y_count, 2, model_width + PAD)
    terms, *cots = pl.pallas_call(
        cotangent_kernel,
        out_shape=(
            pltpu.HBM(terms_shape, BF),
            *[pltpu.HBM((held, block_size, model_width + PAD), BF)] * sharers,
        ),
        in_specs=[smem] * 2 + [vmem] * 5 + [hbm] * (2 + held),
        out_specs=(hbm,) * (1 + sharers),
        scratch_shapes=[pltpu.VMEM((tok_count, model_width), BF)] * 3
        + [
            pltpu.VMEM((tok_count, model_width + PAD), BF),
            pltpu.VMEM(terms_shape, BF),
            pltpu.SemaphoreType.DMA((2,)),
            pltpu.SemaphoreType.DMA((tenant_count + model_width // CHUNK,)),
        ],
        compiler_params=grant,
        name="cotangent",
    )(
        local_ids,
        place,
        returned,
        pick,
        gain[None, :],
        rstd_kept,
        spread,
        pltpu.with_memory_space_constraint(normed, pltpu.HBM),
        pltpu.with_memory_space_constraint(d_out, pltpu.HBM),
        *shards,
    )

    arrived = exchange(terms, ("z", "y"))

    def swap(array, turn):
        pairs = [
            (x * c_count + c, (x ^ (turn >> 1)) * c_count + (c ^ (turn & 1)))
            for x in range(x_count)
            for c in range(c_count)
        ]
        return lax.ppermute(array, ("x", "c"), pairs)

    came = [cots[0]] + [swap(cots[turn], turn) for turn in range(1, sharers)]
    low_shape = jax.ShapeDtypeStruct((held, block_size, rank_size), BF)
    low_parts = pl.pallas_call(
        low_rank_kernel,
        out_shape=(low_shape,) * sharers,
        in_specs=[vmem] * (sharers + held),
        out_specs=(vmem,) * sharers,
        compiler_params=grant,
        cost_estimate=pl.CostEstimate(flops=1 << 20, bytes_accessed=1 << 20, transcendentals=0),
        name="low_rank",
    )(*came, *shards)
    low_blocks = jnp.concatenate(
        [low_parts[0]] + [swap(low_parts[turn], turn) for turn in range(1, sharers)], axis=0
    )
    low_rank_grad = jnp.take(low_blocks, place, axis=0).reshape(tok_count, rank_size)

    column_parts = x_count * c_count
    sums = pl.pallas_call(
        sum_kernel,
        out_shape=jax.ShapeDtypeStruct((column_parts, ten_dev, 2 * model_width // column_parts), F32),
        in_specs=[vmem, pl.BlockSpec(memory_space=pl.ANY)],
        out_specs=vmem,
        compiler_params=grant,
        name="tenant_sums",
    )(arrived, low_rank_grad)
    grad_b = jnp.sum(exchange(sums, ("x", "c")), axis=0)
    return (grad_b, low_rank_grad)


def solution(mesh):
    fine = Mesh(mesh.devices.reshape(8, 8, 4, 2), ALL)
    expert = ("y", "x", "c")
    placed = (
        P(ALL, None),
        P(ALL, None),
        P(ALL),
        P(),
        P("z", expert, None, None, None),
        P(ALL, None),
        P(ALL, None),
        P(ALL),
        P(ALL),
        P("z", None, None),
    )
    return jax.shard_map(
        per_device,
        mesh=fine,
        in_specs=placed,
        out_specs=(P("z", expert), P(ALL, None)),
        check_vma=False,
    )
```

```python
import jax
import jax.numpy as jnp
from jax import lax
from jax.experimental import pallas as pl
from jax.experimental.pallas import tpu as pltpu
from jax.sharding import Mesh
from jax.sharding import PartitionSpec as P

ALL = ("z", "y", "x", "c")
CHUNK = 512
PAD = 128
BF = jnp.bfloat16
F32 = jnp.float32
STEPS = ((0, 4), (1, 7), (2, 6), (3, 5))


def step_of(kind, turn):
    return jnp.where(kind == 0, 4, 8 - kind) if turn else kind


def own_kind():
    return lax.axis_index("x") % 2 * 2 + lax.axis_index("c")


def partner_of(index, x_count):
    return (lax.axis_index("c") ^ (index & 1)) * x_count + (lax.axis_index("x") ^ (index >> 1))


def exchange(array, axes):
    return lax.all_to_all(array, axes, split_axis=0, concat_axis=0, tiled=True)


def cotangent_kernel(
    recv_ref, pick_ref, gain_ref, rstd_ref, spread_ref, marks_ref, cot_marks_ref, normed_hbm, out_grad_hbm, *rest
):
    terms_hbm, *sent_hbm = rest[-12:-7]
    normed_ref, out_grad_ref, moe_ref, cot_ref, terms_ref, in_sems, out_sems = rest[-7:]
    fetch_normed = pltpu.make_async_copy(normed_hbm, normed_ref, in_sems.at[0])
    fetch_out = pltpu.make_async_copy(out_grad_hbm, out_grad_ref, in_sems.at[1])
    fetch_normed.start()
    fetch_out.start()
    tokens, width = normed_ref.shape
    slots = recv_ref.shape[0] * recv_ref.shape[1]
    pairs = terms_ref.shape[0]
    held, block_size, _ = sent_hbm[0].shape
    blocks = tokens // block_size
    pick = pick_ref[...]
    for start in range(0, width, CHUNK):
        cols = slice(start, start + CHUNK)
        rows = recv_ref[:, :, cols].reshape(slots, CHUNK)
        moe_ref[:, cols] = jnp.dot(pick, rows, preferred_element_type=F32).astype(BF)
    terms_ref[:, :, width:] = marks_ref[...]
    cot_ref[:, width:] = cot_marks_ref[...]
    fetch_normed.wait()
    total = None
    for start in range(0, width, CHUNK):
        cols = slice(start, start + CHUNK)
        part = gain_ref[:, cols] * moe_ref[:, cols].astype(F32) * normed_ref[:, cols].astype(F32)
        total = part if total is None else total + part
    centre = jnp.sum(total, axis=1, keepdims=True) * (1.0 / width)
    rstd = rstd_ref[...]
    keep = rstd > 0.0
    spread = spread_ref[...]
    fetch_out.wait()
    stores = []
    for start in range(0, width, CHUNK):
        cols = slice(start, start + CHUNK)
        weighted = gain_ref[:, cols] * moe_ref[:, cols].astype(F32)
        norm_grad = rstd * (weighted - normed_ref[:, cols].astype(F32) * centre)
        cot = jnp.where(keep, out_grad_ref[:, cols].astype(F32) + norm_grad, 0.0).astype(BF)
        cot_ref[:, cols] = cot
        terms = jnp.dot(spread, cot, preferred_element_type=F32).astype(BF)
        terms_ref[:, :, cols] = terms.reshape(pairs, 2, CHUNK)
        last = start + CHUNK == width
        done = pl.ds(start, CHUNK + PAD if last else CHUNK)
        store = pltpu.make_async_copy(
            terms_ref.at[:, :, done], terms_hbm.at[:, :, done], out_sems.at[blocks + len(stores)]
        )
        store.start()
        stores.append(store)

    kind, row = own_kind(), lax.axis_index("z")
    sends = []
    for index, target in enumerate(sent_hbm):
        for turn in range(held):
            block = (step_of(kind ^ index, turn) + row) % blocks
            start = pl.multiple_of(block * block_size, block_size)
            sends.append(
                pltpu.make_async_copy(
                    cot_ref.at[pl.ds(start, block_size), :], target.at[turn], out_sems.at[len(sends)]
                )
            )
    for send in sends:
        send.start()
    for store in stores:
        store.wait()
    for send in sends:
        send.wait()


def low_rank_kernel(*refs):
    sharers = len(STEPS)
    cots, shards, packs_ref = refs[:sharers], refs[sharers:-1], refs[-1]
    block_size = cots[0].shape[1]
    width = cots[0].shape[2] - PAD
    rows_out = packs_ref.shape[1]
    rank = rows_out * packs_ref.shape[2] // (len(shards) * block_size)
    tenants = shards[0].shape[0] // rank
    parts = []
    for turn in range(len(shards)):
        rows = jnp.concatenate([cot[turn, :, :width] for cot in cots], axis=0)
        marks = jnp.concatenate([cot[turn, :, width:] for cot in cots], axis=0).astype(F32)
        projected = lax.dot_general(
            rows, shards[turn][...], (((1,), (1,)), ((), ())), preferred_element_type=F32
        )
        lane = lax.broadcasted_iota(jnp.int32, projected.shape, 1)
        hit = (lane // rank).astype(F32) == marks[:, : tenants * rank]
        chosen = jnp.where(hit, projected, 0.0)
        total = chosen[:, :rank]
        for tenant in range(1, tenants):
            total = total + chosen[:, tenant * rank : (tenant + 1) * rank]
        parts.append(total.T)
    for index in range(sharers):
        cols = slice(index * block_size, (index + 1) * block_size)
        pieces = [
            part[first : first + rows_out, cols] for first in range(0, rank, rows_out) for part in parts
        ]
        packs_ref[index] = jnp.concatenate(pieces, axis=1)


def sum_kernel(terms_ref, packs_ref, sums_ref):
    sources, _, padded = terms_ref.shape
    width = padded - PAD
    quarter = sums_ref.shape[2] - PAD
    tenants = sums_ref.shape[1]
    marks = terms_ref[:, :, width:].reshape(2 * sources, PAD).astype(F32)
    row = lax.broadcasted_iota(jnp.int32, (2 * sources, PAD), 0)
    lane = lax.broadcasted_iota(jnp.int32, (2 * sources, PAD), 1)
    wanted = (lane % tenants).astype(F32)
    hit = (marks == wanted) & (row % 2 == lane // tenants)
    chosen = jnp.where(hit, 1.0, 0.0).astype(BF).T[: 2 * tenants]
    for part in range(width // quarter):
        cols = slice(part * quarter, (part + 1) * quarter)
        rows = terms_ref[:, :, cols].reshape(2 * sources, quarter)
        sums = jnp.dot(chosen, rows, preferred_element_type=F32)
        for row in range(2):
            holder = part % 2 * (width // quarter) + row * 2 + part // 2
            sums_ref[holder, :, :quarter] = sums[row * tenants : (row + 1) * tenants]
    sums_ref[:, :, quarter:] = jnp.zeros((sums_ref.shape[0], tenants, PAD), F32)
    for index in range(packs_ref.shape[0]):
        sums_ref[partner_of(index, sums_ref.shape[0] // 2), :, quarter:] = packs_ref[index]


def finish_kernel(got_ref, grad_ref, low_ref):
    holders, rows_out, padded = got_ref.shape
    width = padded - PAD
    total = got_ref[0, :, :width]
    for holder in range(1, holders):
        total = total + got_ref[holder, :, :width]
    grad_ref[...] = total
    rank, tokens = low_ref.shape
    sharers, held = len(STEPS), len(STEPS[0])
    blocks = sharers * held
    block_size = tokens // blocks
    packs = [got_ref[partner_of(index, holders // 2), :, width:] for index in range(sharers)]
    span = held * block_size
    columns = jnp.concatenate(
        [
            jnp.concatenate([pack[:, group * span : (group + 1) * span] for pack in packs], axis=1)
            for group in range(rank // rows_out)
        ],
        axis=0,
    ).astype(BF)
    row = lax.broadcasted_iota(jnp.int32, (block_size, tokens), 0)
    lane = lax.broadcasted_iota(jnp.int32, (block_size, tokens), 1)
    kind, place = own_kind(), lax.axis_index("z")
    starts = [
        (step_of(kind ^ index, turn) + place) % blocks * block_size
        for index in range(sharers)
        for turn in range(held)
    ]
    moves = jnp.concatenate(
        [jnp.where(lane == start + row, 1.0, 0.0) for start in starts], axis=0
    ).astype(BF)
    low_ref[...] = jnp.dot(columns, moves, preferred_element_type=F32).astype(BF)


def per_device(
    d_out, normed, rstd, gain, expert_grads, expert_ids, low_rank, lengths, tenant_ids, adapters
):
    tok_count, model_width = d_out.shape
    expert_count, slot_count = expert_grads.shape[2], expert_grads.shape[3]
    tenant_count = lax.axis_size("z")
    block_size = tok_count // tenant_count
    ten_dev, rank_size = adapters.shape[0], adapters.shape[1]
    y_count = lax.axis_size("y")

    returned = exchange(expert_grads[0, 0], ("y", "x", "c"))

    x_count, c_count = lax.axis_size("x"), lax.axis_size("c")
    sharers, held = len(STEPS), len(STEPS[0])
    shard = adapters.reshape(ten_dev * rank_size, model_width)
    shards = [
        lax.ppermute(
            shard,
            ("z", "x", "c"),
            [
                (
                    ((z + STEPS[x % 2 * 2 + c][turn]) % tenant_count * x_count + x) * c_count + c,
                    (z * x_count + x) * c_count + c,
                )
                for z in range(tenant_count)
                for x in range(x_count)
                for c in range(c_count)
            ],
        )
        for turn in range(held)
    ]
    local_ids = tenant_ids - jnp.arange(tenant_count, dtype=jnp.int32) * ten_dev
    routes = expert_ids[:, 0]
    onehot = (routes[:, None] == jnp.arange(expert_count, dtype=jnp.int32)[None, :]).astype(F32)
    position = jnp.arange(tok_count, dtype=jnp.int32)
    earlier = (position[:, None] > position[None, :]).astype(F32)
    before = jnp.dot(earlier, onehot, preferred_element_type=F32)
    slot_ids = jnp.sum(before * onehot, axis=1).astype(jnp.int32)
    flat_slot = routes * slot_count + slot_ids
    pick = (
        flat_slot[:, None] == jnp.arange(expert_count * slot_count, dtype=jnp.int32)[None, :]
    ).astype(BF)
    valid = (
        jnp.arange(block_size, dtype=jnp.int32)[None, :] < lengths[:, None]
    ).reshape(tok_count, 1)
    zero = jnp.zeros((), BF)
    rstd_kept = jnp.where(valid, rstd[:, None], 0.0)
    block_of = position // block_size
    low_t = jnp.broadcast_to(
        low_rank.T.reshape(y_count, 1, 2, tok_count), (y_count, tenant_count, 2, tok_count)
    ).reshape(tok_count, tok_count)
    row_block = position // 2 % tenant_count
    spread = jnp.where(row_block[:, None] == block_of[None, :], low_t, zero)
    marks = jnp.broadcast_to(
        local_ids.astype(BF)[None, :, None, None], (y_count, tenant_count, 2, PAD)
    ).reshape(y_count * tenant_count, 2, PAD)
    cot_marks = jnp.broadcast_to(
        local_ids.astype(BF)[:, None, None], (tenant_count, block_size, PAD)
    ).reshape(tok_count, PAD)

    vmem = pl.BlockSpec(memory_space=pltpu.VMEM)
    grant = pltpu.CompilerParams(vmem_limit_bytes=24 * 1024 * 1024)
    hbm = pl.BlockSpec(memory_space=pl.ANY)
    terms_shape = (tenant_count * y_count, 2, model_width + PAD)
    terms, *cots = pl.pallas_call(
        cotangent_kernel,
        out_shape=(
            pltpu.HBM(terms_shape, BF),
            *[pltpu.HBM((held, block_size, model_width + PAD), BF)] * sharers,
        ),
        in_specs=[vmem] * 7 + [hbm] * (2 + held),
        out_specs=(hbm,) * (1 + sharers),
        scratch_shapes=[pltpu.VMEM((tok_count, model_width), BF)] * 3
        + [
            pltpu.VMEM((tok_count, model_width + PAD), BF),
            pltpu.VMEM(terms_shape, BF),
            pltpu.SemaphoreType.DMA((2,)),
            pltpu.SemaphoreType.DMA((tenant_count + model_width // CHUNK,)),
        ],
        compiler_params=grant,
        name="cotangent",
    )(
        returned,
        pick,
        gain[None, :],
        rstd_kept,
        spread,
        marks,
        cot_marks,
        pltpu.with_memory_space_constraint(normed, pltpu.HBM),
        pltpu.with_memory_space_constraint(d_out, pltpu.HBM),
        *shards,
    )

    arrived = exchange(terms, ("y", "z"))

    def swap(array, turn):
        pairs = [
            (x * c_count + c, (x ^ (turn >> 1)) * c_count + (c ^ (turn & 1)))
            for x in range(x_count)
            for c in range(c_count)
        ]
        return lax.ppermute(array, ("x", "c"), pairs)

    came = [cots[0]] + [swap(cots[turn], turn) for turn in range(1, sharers)]
    column_parts = x_count * c_count
    packs = pl.pallas_call(
        low_rank_kernel,
        out_shape=jax.ShapeDtypeStruct((sharers, ten_dev, PAD), F32),
        in_specs=[vmem] * (sharers + held),
        out_specs=vmem,
        compiler_params=grant,
        cost_estimate=pl.CostEstimate(flops=1 << 20, bytes_accessed=1 << 20, transcendentals=0),
        name="low_rank",
    )(*came, *shards)
    sums = pl.pallas_call(
        sum_kernel,
        out_shape=jax.ShapeDtypeStruct(
            (column_parts, ten_dev, 2 * model_width // column_parts + PAD), F32
        ),
        in_specs=[vmem, vmem],
        out_specs=vmem,
        compiler_params=grant,
        name="tenant_sums",
    )(arrived, packs)
    grad_b, low_columns = pl.pallas_call(
        finish_kernel,
        out_shape=(
            jax.ShapeDtypeStruct((ten_dev, 2 * model_width // column_parts), F32),
            jax.ShapeDtypeStruct((rank_size, tok_count), BF),
        ),
        in_specs=[vmem],
        out_specs=(vmem, vmem),
        compiler_params=grant,
        name="finish",
    )(exchange(sums, ("c", "x")))
    return (grad_b, low_columns.T)


def solution(mesh):
    fine = Mesh(mesh.devices.reshape(8, 8, 4, 2), ALL)
    expert = ("y", "x", "c")
    placed = (
        P(ALL, None),
        P(ALL, None),
        P(ALL),
        P(),
        P("z", expert, None, None, None),
        P(ALL, None),
        P(ALL, None),
        P(ALL),
        P(ALL),
        P("z", None, None),
    )
    return jax.shard_map(
        per_device,
        mesh=fine,
        in_specs=placed,
        out_specs=(P("z", expert), P(ALL, None)),
        check_vma=False,
    )
```

```python
import jax
import jax.numpy as jnp
from jax import lax
from jax.experimental import pallas as pl
from jax.experimental.pallas import tpu as pltpu
from jax.sharding import Mesh
from jax.sharding import PartitionSpec as P

ALL = ("z", "y", "x", "c")
CHUNK = 512
PAD = 128
BF = jnp.bfloat16
F32 = jnp.float32
STEPS = ((0, 4), (1, 7), (2, 6), (3, 5))


def step_of(kind, turn):
    return jnp.where(kind == 0, 4, 8 - kind) if turn else kind


def own_kind():
    return lax.axis_index("x") % 2 * 2 + lax.axis_index("c")


def partner_of(index, x_count):
    return (lax.axis_index("c") ^ (index & 1)) * x_count + (lax.axis_index("x") ^ (index >> 1))


def exchange(array, axes):
    return lax.all_to_all(array, axes, split_axis=0, concat_axis=0, tiled=True)


def cotangent_kernel(
    recv_ref, pick_ref, gain_ref, rstd_ref, spread_ref, marks_ref, normed_hbm, out_grad_hbm, *rest
):
    terms_hbm, *sent_hbm = rest[-12:-7]
    normed_ref, out_grad_ref, moe_ref, cot_ref, terms_ref, in_sems, out_sems = rest[-7:]
    fetch_normed = pltpu.make_async_copy(normed_hbm, normed_ref, in_sems.at[0])
    fetch_out = pltpu.make_async_copy(out_grad_hbm, out_grad_ref, in_sems.at[1])
    fetch_normed.start()
    fetch_out.start()
    tokens, width = normed_ref.shape
    slots = recv_ref.shape[0] * recv_ref.shape[1]
    pairs = terms_ref.shape[0]
    held, block_size, _ = sent_hbm[0].shape
    blocks = tokens // block_size
    pick = pick_ref[...]
    for start in range(0, width, CHUNK):
        cols = slice(start, start + CHUNK)
        rows = recv_ref[:, :, cols].reshape(slots, CHUNK)
        moe_ref[:, cols] = jnp.dot(pick, rows, preferred_element_type=F32).astype(BF)
    terms_ref[:, :, width:] = marks_ref[...]
    for block in range(blocks):
        rows = slice(block * block_size, (block + 1) * block_size)
        cot_ref[rows, width:] = jnp.broadcast_to(marks_ref[block, :1, :], (block_size, PAD))
    fetch_normed.wait()
    total = None
    for start in range(0, width, CHUNK):
        cols = slice(start, start + CHUNK)
        part = gain_ref[:, cols] * moe_ref[:, cols].astype(F32) * normed_ref[:, cols].astype(F32)
        total = part if total is None else total + part
    centre = jnp.sum(total, axis=1, keepdims=True) * (1.0 / width)
    rstd = rstd_ref[...]
    keep = rstd > 0.0
    spread = spread_ref[...]
    fetch_out.wait()
    stores = []
    for start in range(0, width, CHUNK):
        cols = slice(start, start + CHUNK)
        weighted = gain_ref[:, cols] * moe_ref[:, cols].astype(F32)
        norm_grad = rstd * (weighted - normed_ref[:, cols].astype(F32) * centre)
        cot = jnp.where(keep, out_grad_ref[:, cols].astype(F32) + norm_grad, 0.0).astype(BF)
        cot_ref[:, cols] = cot
        terms = jnp.dot(spread, cot, preferred_element_type=F32).astype(BF)
        terms_ref[:, :, cols] = terms.reshape(pairs, 2, CHUNK)
        last = start + CHUNK == width
        done = pl.ds(start, CHUNK + PAD if last else CHUNK)
        store = pltpu.make_async_copy(
            terms_ref.at[:, :, done], terms_hbm.at[:, :, done], out_sems.at[blocks + len(stores)]
        )
        store.start()
        stores.append(store)

    kind, row = own_kind(), lax.axis_index("z")
    sends = []
    for index, target in enumerate(sent_hbm):
        for turn in range(held):
            block = (step_of(kind ^ index, turn) + row) % blocks
            start = pl.multiple_of(block * block_size, block_size)
            sends.append(
                pltpu.make_async_copy(
                    cot_ref.at[pl.ds(start, block_size), :], target.at[turn], out_sems.at[len(sends)]
                )
            )
    for send in sends:
        send.start()
    for store in stores:
        store.wait()
    for send in sends:
        send.wait()


def low_rank_kernel(*refs):
    sharers = len(STEPS)
    cots, shards, packs_ref = refs[:sharers], refs[sharers:-1], refs[-1]
    block_size = cots[0].shape[1]
    width = cots[0].shape[2] - PAD
    rows_out = packs_ref.shape[1]
    rank = rows_out * packs_ref.shape[2] // (len(shards) * block_size)
    tenants = shards[0].shape[0] // rank
    parts = []
    for turn in range(len(shards)):
        rows = jnp.concatenate([cot[turn, :, :width] for cot in cots], axis=0)
        marks = jnp.concatenate([cot[turn, :, width:] for cot in cots], axis=0).astype(F32)
        projected = lax.dot_general(
            rows, shards[turn][...], (((1,), (1,)), ((), ())), preferred_element_type=F32
        )
        lane = lax.broadcasted_iota(jnp.int32, projected.shape, 1)
        hit = (lane // rank).astype(F32) == marks[:, : tenants * rank]
        chosen = jnp.where(hit, projected, 0.0)
        total = chosen[:, :rank]
        for tenant in range(1, tenants):
            total = total + chosen[:, tenant * rank : (tenant + 1) * rank]
        parts.append(total.T)
    for index in range(sharers):
        cols = slice(index * block_size, (index + 1) * block_size)
        pieces = [
            part[first : first + rows_out, cols] for first in range(0, rank, rows_out) for part in parts
        ]
        packs_ref[index] = jnp.concatenate(pieces, axis=1).astype(BF)


def sum_kernel(terms_ref, packs_ref, sums_ref):
    sources, _, padded = terms_ref.shape
    width = padded - PAD
    quarter = sums_ref.shape[2] - PAD
    tenants = sums_ref.shape[1]
    marks = terms_ref[:, :, width:].reshape(2 * sources, PAD).astype(F32)
    row = lax.broadcasted_iota(jnp.int32, (2 * sources, PAD), 0)
    lane = lax.broadcasted_iota(jnp.int32, (2 * sources, PAD), 1)
    wanted = (lane % tenants).astype(F32)
    hit = (marks == wanted) & (row % 2 == lane // tenants)
    chosen = jnp.where(hit, 1.0, 0.0).astype(BF).T[: 2 * tenants]
    for part in range(width // quarter):
        cols = slice(part * quarter, (part + 1) * quarter)
        rows = terms_ref[:, :, cols].reshape(2 * sources, quarter)
        sums = jnp.dot(chosen, rows, preferred_element_type=F32)
        for row in range(2):
            holder = part % 2 * (width // quarter) + row * 2 + part // 2
            sums_ref[holder, :, :quarter] = sums[row * tenants : (row + 1) * tenants].astype(BF)
    sums_ref[:, :, quarter:] = jnp.zeros((sums_ref.shape[0], tenants, PAD), BF)
    for index in range(packs_ref.shape[0]):
        sums_ref[partner_of(index, sums_ref.shape[0] // 2), :, quarter:] = packs_ref[index]


def finish_kernel(got_ref, grad_ref, low_ref):
    holders, rows_out, padded = got_ref.shape
    width = padded - PAD
    total = got_ref[0, :, :width].astype(F32)
    for holder in range(1, holders):
        total = total + got_ref[holder, :, :width].astype(F32)
    grad_ref[...] = total
    rank, tokens = low_ref.shape
    sharers, held = len(STEPS), len(STEPS[0])
    blocks = sharers * held
    block_size = tokens // blocks
    packs = [
        got_ref[partner_of(index, holders // 2), :, width:].astype(F32) for index in range(sharers)
    ]
    span = held * block_size
    columns = jnp.concatenate(
        [
            jnp.concatenate([pack[:, group * span : (group + 1) * span] for pack in packs], axis=1)
            for group in range(rank // rows_out)
        ],
        axis=0,
    ).astype(BF)
    row = lax.broadcasted_iota(jnp.int32, (block_size, tokens), 0)
    lane = lax.broadcasted_iota(jnp.int32, (block_size, tokens), 1)
    kind, place = own_kind(), lax.axis_index("z")
    starts = [
        (step_of(kind ^ index, turn) + place) % blocks * block_size
        for index in range(sharers)
        for turn in range(held)
    ]
    moves = jnp.concatenate(
        [jnp.where(lane == start + row, 1.0, 0.0) for start in starts], axis=0
    ).astype(BF)
    low_ref[...] = jnp.dot(columns, moves, preferred_element_type=F32).astype(BF)


def per_device(
    d_out, normed, rstd, gain, expert_grads, expert_ids, low_rank, lengths, tenant_ids, adapters
):
    tok_count, model_width = d_out.shape
    expert_count, slot_count = expert_grads.shape[2], expert_grads.shape[3]
    tenant_count = lax.axis_size("z")
    block_size = tok_count // tenant_count
    ten_dev, rank_size = adapters.shape[0], adapters.shape[1]
    y_count = lax.axis_size("y")

    returned = exchange(expert_grads[0, 0], ("y", "x", "c"))

    x_count, c_count = lax.axis_size("x"), lax.axis_size("c")
    sharers, held = len(STEPS), len(STEPS[0])
    shard = adapters.reshape(ten_dev * rank_size, model_width)
    shards = [
        lax.ppermute(
            shard,
            ("z", "x", "c"),
            [
                (
                    ((z + STEPS[x % 2 * 2 + c][turn]) % tenant_count * x_count + x) * c_count + c,
                    (z * x_count + x) * c_count + c,
                )
                for z in range(tenant_count)
                for x in range(x_count)
                for c in range(c_count)
            ],
        )
        for turn in range(held)
    ]
    local_ids = tenant_ids - jnp.arange(tenant_count, dtype=jnp.int32) * ten_dev
    routes = expert_ids[:, 0]
    onehot = (routes[:, None] == jnp.arange(expert_count, dtype=jnp.int32)[None, :]).astype(F32)
    position = jnp.arange(tok_count, dtype=jnp.int32)
    earlier = (position[:, None] > position[None, :]).astype(F32)
    before = jnp.dot(earlier, onehot, preferred_element_type=F32)
    slot_ids = jnp.sum(before * onehot, axis=1).astype(jnp.int32)
    flat_slot = routes * slot_count + slot_ids
    pick = (
        flat_slot[:, None] == jnp.arange(expert_count * slot_count, dtype=jnp.int32)[None, :]
    ).astype(BF)
    valid = (
        jnp.arange(block_size, dtype=jnp.int32)[None, :] < lengths[:, None]
    ).reshape(tok_count, 1)
    zero = jnp.zeros((), BF)
    rstd_kept = jnp.where(valid, rstd[:, None], 0.0)
    block_of = position // block_size
    low_t = jnp.broadcast_to(
        low_rank.T.reshape(y_count, 1, 2, tok_count), (y_count, tenant_count, 2, tok_count)
    ).reshape(tok_count, tok_count)
    row_block = position // 2 % tenant_count
    spread = jnp.where(row_block[:, None] == block_of[None, :], low_t, zero)
    marks = jnp.broadcast_to(
        local_ids.astype(BF)[None, :, None, None], (y_count, tenant_count, 2, PAD)
    ).reshape(y_count * tenant_count, 2, PAD)

    vmem = pl.BlockSpec(memory_space=pltpu.VMEM)
    grant = pltpu.CompilerParams(vmem_limit_bytes=24 * 1024 * 1024)
    hbm = pl.BlockSpec(memory_space=pl.ANY)
    terms_shape = (tenant_count * y_count, 2, model_width + PAD)
    terms, *cots = pl.pallas_call(
        cotangent_kernel,
        out_shape=(
            pltpu.HBM(terms_shape, BF),
            *[pltpu.HBM((held, block_size, model_width + PAD), BF)] * sharers,
        ),
        in_specs=[vmem] * 6 + [hbm] * (2 + held),
        out_specs=(hbm,) * (1 + sharers),
        scratch_shapes=[pltpu.VMEM((tok_count, model_width), BF)] * 3
        + [
            pltpu.VMEM((tok_count, model_width + PAD), BF),
            pltpu.VMEM(terms_shape, BF),
            pltpu.SemaphoreType.DMA((2,)),
            pltpu.SemaphoreType.DMA((tenant_count + model_width // CHUNK,)),
        ],
        compiler_params=grant,
        name="cotangent",
    )(
        returned,
        pick,
        gain[None, :],
        rstd_kept,
        spread,
        marks,
        pltpu.with_memory_space_constraint(normed, pltpu.HBM),
        pltpu.with_memory_space_constraint(d_out, pltpu.HBM),
        *shards,
    )

    arrived = exchange(terms, ("y", "z"))

    def swap(array, turn):
        pairs = [
            (x * c_count + c, (x ^ (turn >> 1)) * c_count + (c ^ (turn & 1)))
            for x in range(x_count)
            for c in range(c_count)
        ]
        return lax.ppermute(array, ("x", "c"), pairs)

    came = [cots[0]] + [swap(cots[turn], turn) for turn in range(1, sharers)]
    column_parts = x_count * c_count
    packs = pl.pallas_call(
        low_rank_kernel,
        out_shape=jax.ShapeDtypeStruct((sharers, ten_dev, PAD), BF),
        in_specs=[vmem] * (sharers + held),
        out_specs=vmem,
        compiler_params=grant,
        cost_estimate=pl.CostEstimate(flops=1 << 20, bytes_accessed=1 << 20, transcendentals=0),
        name="low_rank",
    )(*came, *shards)
    sums = pl.pallas_call(
        sum_kernel,
        out_shape=jax.ShapeDtypeStruct(
            (column_parts, ten_dev, 2 * model_width // column_parts + PAD), BF
        ),
        in_specs=[vmem, vmem],
        out_specs=vmem,
        compiler_params=grant,
        name="tenant_sums",
    )(arrived, packs)
    grad_b, low_columns = pl.pallas_call(
        finish_kernel,
        out_shape=(
            jax.ShapeDtypeStruct((ten_dev, 2 * model_width // column_parts), F32),
            jax.ShapeDtypeStruct((rank_size, tok_count), BF),
        ),
        in_specs=[vmem],
        out_specs=(vmem, vmem),
        compiler_params=grant,
        name="finish",
    )(exchange(sums, ("c", "x")))
    return (grad_b, low_columns.T)


def solution(mesh):
    fine = Mesh(mesh.devices.reshape(8, 8, 4, 2), ALL)
    expert = ("y", "x", "c")
    placed = (
        P(ALL, None),
        P(ALL, None),
        P(ALL),
        P(),
        P("z", expert, None, None, None),
        P(ALL, None),
        P(ALL, None),
        P(ALL),
        P(ALL),
        P("z", None, None),
    )
    return jax.shard_map(
        per_device,
        mesh=fine,
        in_specs=placed,
        out_specs=(P("z", expert), P(ALL, None)),
        check_vma=False,
    )
```

```python
import jax
import jax.numpy as jnp
from jax import lax
from jax.experimental import pallas as pl
from jax.experimental.pallas import tpu as pltpu
from jax.sharding import Mesh
from jax.sharding import PartitionSpec as P

ALL = ("z", "y", "x", "c")
CHUNK = 512
PAD = 128
PIECES = 4
BF = jnp.bfloat16
F32 = jnp.float32
STEPS = ((0, 4), (1, 7), (2, 6), (3, 5))


def step_of(kind, turn):
    return jnp.where(kind == 0, 4, 8 - kind) if turn else kind


def own_kind():
    return lax.axis_index("x") % 2 * 2 + lax.axis_index("c")


def partner_of(index, x_count):
    return (lax.axis_index("c") ^ (index & 1)) * x_count + (lax.axis_index("x") ^ (index >> 1))


def exchange(array, axes):
    return lax.all_to_all(array, axes, split_axis=0, concat_axis=0, tiled=True)


def cotangent_kernel(
    recv_ref, pick_ref, gain_ref, rstd_ref, spread_ref, marks_ref, normed_ref, out_grad_hbm, *rest
):
    terms_hbm, *sent_hbm = rest[-11:-6]
    out_grad_ref, moe_ref, cot_ref, terms_ref, in_sems, out_sems = rest[-6:]
    step = out_grad_ref.shape[0] // PIECES
    fetches = []
    for piece in range(PIECES):
        here = pl.ds(piece * step, step)
        fetches.append(
            pltpu.make_async_copy(out_grad_hbm.at[here, :], out_grad_ref.at[here, :], in_sems.at[piece])
        )
    for fetch in fetches:
        fetch.start()
    tokens, width = normed_ref.shape
    slots = recv_ref.shape[0] * recv_ref.shape[1]
    pairs = terms_ref.shape[0]
    held, block_size, _ = sent_hbm[0].shape
    blocks = tokens // block_size
    pick = pick_ref[...]
    total = None
    for start in range(0, width, CHUNK):
        cols = slice(start, start + CHUNK)
        rows = recv_ref[:, :, cols].reshape(slots, CHUNK)
        moe = jnp.dot(pick, rows, preferred_element_type=F32)
        moe_ref[:, cols] = moe.astype(BF)
        part = gain_ref[:, cols] * moe * normed_ref[:, cols].astype(F32)
        total = part if total is None else total + part
    terms_ref[:, :, width:] = marks_ref[...]
    for block in range(blocks):
        rows = slice(block * block_size, (block + 1) * block_size)
        cot_ref[rows, width:] = jnp.broadcast_to(marks_ref[block, :1, :], (block_size, PAD))
    centre = jnp.sum(total, axis=1, keepdims=True) * (1.0 / width)
    rstd = rstd_ref[...]
    keep = rstd > 0.0
    spread = spread_ref[...]
    for piece, fetch in enumerate(fetches):
        fetch.wait()
        here = slice(piece * step, (piece + 1) * step)
        for start in range(0, width, CHUNK):
            cols = slice(start, start + CHUNK)
            weighted = gain_ref[:, cols] * moe_ref[here, cols].astype(F32)
            norm_grad = rstd[here] * (weighted - normed_ref[here, cols].astype(F32) * centre[here])
            added = out_grad_ref[here, cols].astype(F32) + norm_grad
            cot_ref[here, cols] = jnp.where(keep[here], added, 0.0).astype(BF)
    kind, row = own_kind(), lax.axis_index("z")
    sends = []
    for index, target in enumerate(sent_hbm):
        for turn in range(held):
            block = (step_of(kind ^ index, turn) + row) % blocks
            start = pl.multiple_of(block * block_size, block_size)
            sends.append(
                pltpu.make_async_copy(
                    cot_ref.at[pl.ds(start, block_size), :], target.at[turn], out_sems.at[len(sends)]
                )
            )
    for send in sends:
        send.start()
    stores = []
    for start in range(0, width, CHUNK):
        cols = slice(start, start + CHUNK)
        cot = cot_ref[:, cols]
        terms = jnp.dot(spread, cot, preferred_element_type=F32).astype(BF)
        terms_ref[:, :, cols] = terms.reshape(pairs, 2, CHUNK)
        last = start + CHUNK == width
        done = pl.ds(start, CHUNK + PAD if last else CHUNK)
        store = pltpu.make_async_copy(
            terms_ref.at[:, :, done], terms_hbm.at[:, :, done], out_sems.at[blocks + len(stores)]
        )
        store.start()
        stores.append(store)
    for store in stores:
        store.wait()
    for send in sends:
        send.wait()


def low_rank_kernel(*refs):
    sharers = len(STEPS)
    held = len(STEPS[0])
    cots, shards_hbm, packs_ref = refs[:sharers], refs[sharers : sharers + held], refs[sharers + held]
    shards, sems = refs[-1 - held : -1], refs[-1]
    fetches = [
        pltpu.make_async_copy(source, target, sems.at[turn])
        for turn, (source, target) in enumerate(zip(shards_hbm, shards))
    ]
    for fetch in fetches:
        fetch.start()
    block_size = cots[0].shape[1]
    width = cots[0].shape[2] - PAD
    rows_out = packs_ref.shape[1]
    rank = rows_out * packs_ref.shape[2] // (len(shards) * block_size)
    tenants = shards[0].shape[0] // rank
    parts = []
    for turn in range(len(shards)):
        fetches[turn].wait()
        rows = jnp.concatenate([cot[turn, :, :width] for cot in cots], axis=0)
        marks = jnp.concatenate([cot[turn, :, width:] for cot in cots], axis=0).astype(F32)
        projected = lax.dot_general(
            rows, shards[turn][...], (((1,), (1,)), ((), ())), preferred_element_type=F32
        )
        lane = lax.broadcasted_iota(jnp.int32, projected.shape, 1)
        hit = (lane // rank).astype(F32) == marks[:, : tenants * rank]
        chosen = jnp.where(hit, projected, 0.0)
        total = chosen[:, :rank]
        for tenant in range(1, tenants):
            total = total + chosen[:, tenant * rank : (tenant + 1) * rank]
        parts.append(total.T)
    for index in range(sharers):
        cols = slice(index * block_size, (index + 1) * block_size)
        pieces = [
            part[first : first + rows_out, cols] for first in range(0, rank, rows_out) for part in parts
        ]
        packs_ref[index] = jnp.concatenate(pieces, axis=1).astype(BF)


def sum_kernel(terms_ref, packs_ref, sums_ref):
    sources, _, padded = terms_ref.shape
    width = padded - PAD
    quarter = sums_ref.shape[2] - PAD
    tenants = sums_ref.shape[1]
    marks = terms_ref[:, :, width:].reshape(2 * sources, PAD).astype(F32)
    row = lax.broadcasted_iota(jnp.int32, (2 * sources, PAD), 0)
    lane = lax.broadcasted_iota(jnp.int32, (2 * sources, PAD), 1)
    wanted = (lane % tenants).astype(F32)
    hit = (marks == wanted) & (row % 2 == lane // tenants)
    chosen = jnp.where(hit, 1.0, 0.0).astype(BF).T[: 2 * tenants]
    for part in range(width // quarter):
        cols = slice(part * quarter, (part + 1) * quarter)
        rows = terms_ref[:, :, cols].reshape(2 * sources, quarter)
        sums = jnp.dot(chosen, rows, preferred_element_type=F32)
        for row in range(2):
            holder = part % 2 * (width // quarter) + row * 2 + part // 2
            sums_ref[holder, :, :quarter] = sums[row * tenants : (row + 1) * tenants].astype(BF)
    sums_ref[:, :, quarter:] = jnp.zeros((sums_ref.shape[0], tenants, PAD), BF)
    for index in range(packs_ref.shape[0]):
        sums_ref[partner_of(index, sums_ref.shape[0] // 2), :, quarter:] = packs_ref[index]


def finish_kernel(got_ref, grad_ref, low_ref):
    holders, rows_out, padded = got_ref.shape
    width = padded - PAD
    total = got_ref[0, :, :width].astype(F32)
    for holder in range(1, holders):
        total = total + got_ref[holder, :, :width].astype(F32)
    grad_ref[...] = total
    rank, tokens = low_ref.shape
    sharers, held = len(STEPS), len(STEPS[0])
    blocks = sharers * held
    block_size = tokens // blocks
    packs = [
        got_ref[partner_of(index, holders // 2), :, width:].astype(F32) for index in range(sharers)
    ]
    span = held * block_size
    columns = jnp.concatenate(
        [
            jnp.concatenate([pack[:, group * span : (group + 1) * span] for pack in packs], axis=1)
            for group in range(rank // rows_out)
        ],
        axis=0,
    ).astype(BF)
    row = lax.broadcasted_iota(jnp.int32, (block_size, tokens), 0)
    lane = lax.broadcasted_iota(jnp.int32, (block_size, tokens), 1)
    kind, place = own_kind(), lax.axis_index("z")
    starts = [
        (step_of(kind ^ index, turn) + place) % blocks * block_size
        for index in range(sharers)
        for turn in range(held)
    ]
    moves = jnp.concatenate(
        [jnp.where(lane == start + row, 1.0, 0.0) for start in starts], axis=0
    ).astype(BF)
    low_ref[...] = jnp.dot(columns, moves, preferred_element_type=F32).astype(BF)


def per_device(
    d_out, normed, rstd, gain, expert_grads, expert_ids, low_rank, lengths, tenant_ids, adapters
):
    tok_count, model_width = d_out.shape
    expert_count, slot_count = expert_grads.shape[2], expert_grads.shape[3]
    tenant_count = lax.axis_size("z")
    block_size = tok_count // tenant_count
    ten_dev, rank_size = adapters.shape[0], adapters.shape[1]
    y_count = lax.axis_size("y")

    returned = exchange(expert_grads[0, 0], ("y", "x", "c"))

    x_count, c_count = lax.axis_size("x"), lax.axis_size("c")
    sharers, held = len(STEPS), len(STEPS[0])
    shard = adapters.reshape(ten_dev * rank_size, model_width)
    shards = [
        lax.ppermute(
            shard,
            ("z", "x", "c"),
            [
                (
                    ((z + STEPS[x % 2 * 2 + c][turn]) % tenant_count * x_count + x) * c_count + c,
                    (z * x_count + x) * c_count + c,
                )
                for z in range(tenant_count)
                for x in range(x_count)
                for c in range(c_count)
            ],
        )
        for turn in range(held)
    ]
    shards = [pltpu.with_memory_space_constraint(array, pltpu.HBM) for array in shards]
    local_ids = tenant_ids - jnp.arange(tenant_count, dtype=jnp.int32) * ten_dev
    routes = expert_ids[:, 0]
    onehot = (routes[:, None] == jnp.arange(expert_count, dtype=jnp.int32)[None, :]).astype(F32)
    position = jnp.arange(tok_count, dtype=jnp.int32)
    earlier = (position[:, None] > position[None, :]).astype(F32)
    before = jnp.dot(earlier, onehot, preferred_element_type=F32)
    slot_ids = jnp.sum(before * onehot, axis=1).astype(jnp.int32)
    flat_slot = routes * slot_count + slot_ids
    pick = (
        flat_slot[:, None] == jnp.arange(expert_count * slot_count, dtype=jnp.int32)[None, :]
    ).astype(BF)
    valid = (
        jnp.arange(block_size, dtype=jnp.int32)[None, :] < lengths[:, None]
    ).reshape(tok_count, 1)
    zero = jnp.zeros((), BF)
    rstd_kept = jnp.where(valid, rstd[:, None], 0.0)
    normed_kept = jnp.where(valid, normed, zero)
    block_of = position // block_size
    low_t = jnp.broadcast_to(
        low_rank.T.reshape(y_count, 1, 2, tok_count), (y_count, tenant_count, 2, tok_count)
    ).reshape(tok_count, tok_count)
    row_block = position // 2 % tenant_count
    spread = jnp.where(row_block[:, None] == block_of[None, :], low_t, zero)
    marks = jnp.broadcast_to(
        local_ids.astype(BF)[None, :, None, None], (y_count, tenant_count, 2, PAD)
    ).reshape(y_count * tenant_count, 2, PAD)

    vmem = pl.BlockSpec(memory_space=pltpu.VMEM)
    grant = pltpu.CompilerParams(vmem_limit_bytes=24 * 1024 * 1024)
    hbm = pl.BlockSpec(memory_space=pl.ANY)
    terms_shape = (tenant_count * y_count, 2, model_width + PAD)
    terms, *cots = pl.pallas_call(
        cotangent_kernel,
        out_shape=(
            pltpu.HBM(terms_shape, BF),
            *[pltpu.HBM((held, block_size, model_width + PAD), BF)] * sharers,
        ),
        in_specs=[vmem] * 7 + [hbm] * (1 + held),
        out_specs=(hbm,) * (1 + sharers),
        scratch_shapes=[pltpu.VMEM((tok_count, model_width), BF)] * 2
        + [
            pltpu.VMEM((tok_count, model_width + PAD), BF),
            pltpu.VMEM(terms_shape, BF),
            pltpu.SemaphoreType.DMA((PIECES,)),
            pltpu.SemaphoreType.DMA((tenant_count + model_width // CHUNK,)),
        ],
        compiler_params=grant,
        name="cotangent",
    )(
        returned,
        pick,
        gain[None, :],
        rstd_kept,
        spread,
        marks,
        normed_kept,
        pltpu.with_memory_space_constraint(d_out, pltpu.HBM),
        *shards,
    )

    arrived = exchange(terms, ("y", "z"))

    def swap(array, turn):
        pairs = [
            (x * c_count + c, (x ^ (turn >> 1)) * c_count + (c ^ (turn & 1)))
            for x in range(x_count)
            for c in range(c_count)
        ]
        return lax.ppermute(array, ("x", "c"), pairs)

    came = [cots[0]] + [swap(cots[turn], turn) for turn in range(1, sharers)]
    column_parts = x_count * c_count
    packs = pl.pallas_call(
        low_rank_kernel,
        out_shape=jax.ShapeDtypeStruct((sharers, ten_dev, PAD), BF),
        in_specs=[vmem] * sharers + [hbm] * held,
        out_specs=vmem,
        scratch_shapes=[pltpu.VMEM(shard.shape, BF)] * held + [pltpu.SemaphoreType.DMA((held,))],
        compiler_params=grant,
        cost_estimate=pl.CostEstimate(flops=1 << 20, bytes_accessed=1 << 20, transcendentals=0),
        name="low_rank",
    )(*came, *shards)
    sums = pl.pallas_call(
        sum_kernel,
        out_shape=jax.ShapeDtypeStruct(
            (column_parts, ten_dev, 2 * model_width // column_parts + PAD), BF
        ),
        in_specs=[vmem, vmem],
        out_specs=vmem,
        compiler_params=grant,
        name="tenant_sums",
    )(arrived, packs)
    grad_b, low_columns = pl.pallas_call(
        finish_kernel,
        out_shape=(
            jax.ShapeDtypeStruct((ten_dev, 2 * model_width // column_parts), F32),
            jax.ShapeDtypeStruct((rank_size, tok_count), BF),
        ),
        in_specs=[vmem],
        out_specs=(vmem, vmem),
        compiler_params=grant,
        name="finish",
    )(exchange(sums, ("c", "x")))
    return (grad_b, low_columns.T)


def solution(mesh):
    fine = Mesh(mesh.devices.reshape(8, 8, 4, 2), ALL)
    expert = ("y", "x", "c")
    placed = (
        P(ALL, None),
        P(ALL, None),
        P(ALL),
        P(),
        P("z", expert, None, None, None),
        P(ALL, None),
        P(ALL, None),
        P(ALL),
        P(ALL),
        P("z", None, None),
    )
    return jax.shard_map(
        per_device,
        mesh=fine,
        in_specs=placed,
        out_specs=(P("z", expert), P(ALL, None)),
        check_vma=False,
    )
```

```python
import jax
import jax.numpy as jnp
from jax import lax
from jax.experimental import pallas as pl
from jax.experimental.pallas import tpu as pltpu
from jax.sharding import Mesh
from jax.sharding import PartitionSpec as P

ALL = ("z", "y", "x", "c")
CHUNK = 512
PAD = 128
PIECES = 4
BF = jnp.bfloat16
F32 = jnp.float32
STEPS = ((0, 4), (1, 7), (2, 6), (3, 5))


def step_of(kind, turn):
    return jnp.where(kind == 0, 4, 8 - kind) if turn else kind


def own_kind():
    return lax.axis_index("x") % 2 * 2 + lax.axis_index("c")


def partner_of(index, x_count):
    return (lax.axis_index("c") ^ (index & 1)) * x_count + (lax.axis_index("x") ^ (index >> 1))


def exchange(array, axes):
    return lax.all_to_all(array, axes, split_axis=0, concat_axis=0, tiled=True)


def cotangent_kernel(
    recv_ref, pick_ref, gain_ref, rstd_ref, spread_ref, normed_ref, out_grad_hbm, *rest
):
    terms_hbm, *sent_hbm = rest[-11:-6]
    out_grad_ref, moe_ref, cot_ref, terms_ref, in_sems, out_sems = rest[-6:]
    step = out_grad_ref.shape[0] // PIECES
    fetches = []
    for piece in range(PIECES):
        here = pl.ds(piece * step, step)
        fetches.append(
            pltpu.make_async_copy(out_grad_hbm.at[here, :], out_grad_ref.at[here, :], in_sems.at[piece])
        )
    for fetch in fetches:
        fetch.start()
    tokens, width = normed_ref.shape
    slots = recv_ref.shape[0] * recv_ref.shape[1]
    pairs = terms_ref.shape[0]
    held, block_size, _ = sent_hbm[0].shape
    blocks = tokens // block_size
    pick = pick_ref[...]
    total = None
    for start in range(0, width, CHUNK):
        cols = slice(start, start + CHUNK)
        rows = recv_ref[:, :, cols].reshape(slots, CHUNK)
        moe = jnp.dot(pick, rows, preferred_element_type=F32)
        moe_ref[:, cols] = moe.astype(BF)
        part = gain_ref[:, cols] * moe * normed_ref[:, cols].astype(F32)
        total = part if total is None else total + part
    terms_ref[:, :, width:] = spread_ref[:, tokens:].reshape(pairs, 2, PAD)
    for block in range(blocks):
        rows = slice(block * block_size, (block + 1) * block_size)
        cot_ref[rows, width:] = jnp.broadcast_to(
            spread_ref[2 * block : 2 * block + 1, tokens:], (block_size, PAD)
        )
    centre = jnp.sum(total, axis=1, keepdims=True) * (1.0 / width)
    rstd = rstd_ref[...]
    keep = rstd > 0.0
    spread = spread_ref[:, :tokens]
    for piece, fetch in enumerate(fetches):
        fetch.wait()
        here = slice(piece * step, (piece + 1) * step)
        for start in range(0, width, CHUNK):
            cols = slice(start, start + CHUNK)
            weighted = gain_ref[:, cols] * moe_ref[here, cols].astype(F32)
            norm_grad = rstd[here] * (weighted - normed_ref[here, cols].astype(F32) * centre[here])
            added = out_grad_ref[here, cols].astype(F32) + norm_grad
            cot_ref[here, cols] = jnp.where(keep[here], added, 0.0).astype(BF)
    kind, row = own_kind(), lax.axis_index("z")
    sends = []
    for index, target in enumerate(sent_hbm):
        for turn in range(held):
            block = (step_of(kind ^ index, turn) + row) % blocks
            start = pl.multiple_of(block * block_size, block_size)
            sends.append(
                pltpu.make_async_copy(
                    cot_ref.at[pl.ds(start, block_size), :], target.at[turn], out_sems.at[len(sends)]
                )
            )
    for send in sends:
        send.start()
    stores = []
    for start in range(0, width, CHUNK):
        cols = slice(start, start + CHUNK)
        cot = cot_ref[:, cols]
        terms = jnp.dot(spread, cot, preferred_element_type=F32).astype(BF)
        terms_ref[:, :, cols] = terms.reshape(pairs, 2, CHUNK)
        last = start + CHUNK == width
        done = pl.ds(start, CHUNK + PAD if last else CHUNK)
        store = pltpu.make_async_copy(
            terms_ref.at[:, :, done], terms_hbm.at[:, :, done], out_sems.at[blocks + len(stores)]
        )
        store.start()
        stores.append(store)
    for store in stores:
        store.wait()
    for send in sends:
        send.wait()


def low_rank_kernel(*refs):
    sharers = len(STEPS)
    held = len(STEPS[0])
    cots, shards_hbm, packs_ref = refs[:sharers], refs[sharers : sharers + held], refs[sharers + held]
    shards, sems = refs[-1 - held : -1], refs[-1]
    fetches = [
        pltpu.make_async_copy(source, target, sems.at[turn])
        for turn, (source, target) in enumerate(zip(shards_hbm, shards))
    ]
    for fetch in fetches:
        fetch.start()
    block_size = cots[0].shape[1]
    width = cots[0].shape[2] - PAD
    rows_out = packs_ref.shape[1]
    rank = rows_out * packs_ref.shape[2] // (len(shards) * block_size)
    tenants = shards[0].shape[0] // rank
    parts = []
    for turn in range(len(shards)):
        fetches[turn].wait()
        rows = jnp.concatenate([cot[turn, :, :width] for cot in cots], axis=0)
        marks = jnp.concatenate([cot[turn, :, width:] for cot in cots], axis=0).astype(F32)
        projected = lax.dot_general(
            rows, shards[turn][...], (((1,), (1,)), ((), ())), preferred_element_type=F32
        )
        lane = lax.broadcasted_iota(jnp.int32, projected.shape, 1)
        hit = (lane // rank).astype(F32) == marks[:, : tenants * rank]
        chosen = jnp.where(hit, projected, 0.0)
        total = chosen[:, :rank]
        for tenant in range(1, tenants):
            total = total + chosen[:, tenant * rank : (tenant + 1) * rank]
        parts.append(total.T)
    for index in range(sharers):
        cols = slice(index * block_size, (index + 1) * block_size)
        pieces = [
            part[first : first + rows_out, cols] for first in range(0, rank, rows_out) for part in parts
        ]
        packs_ref[index] = jnp.concatenate(pieces, axis=1).astype(BF)


def sum_kernel(terms_ref, packs_ref, sums_ref):
    sources, _, padded = terms_ref.shape
    width = padded - PAD
    quarter = sums_ref.shape[2] - PAD
    tenants = sums_ref.shape[1]
    marks = terms_ref[:, :, width:].reshape(2 * sources, PAD).astype(F32)
    row = lax.broadcasted_iota(jnp.int32, (2 * sources, PAD), 0)
    lane = lax.broadcasted_iota(jnp.int32, (2 * sources, PAD), 1)
    wanted = (lane % tenants).astype(F32)
    hit = (marks == wanted) & (row % 2 == lane // tenants)
    chosen = jnp.where(hit, 1.0, 0.0).astype(BF).T[: 2 * tenants]
    for part in range(width // quarter):
        cols = slice(part * quarter, (part + 1) * quarter)
        rows = terms_ref[:, :, cols].reshape(2 * sources, quarter)
        sums = jnp.dot(chosen, rows, preferred_element_type=F32)
        for row in range(2):
            holder = part % 2 * (width // quarter) + row * 2 + part // 2
            sums_ref[holder, :, :quarter] = sums[row * tenants : (row + 1) * tenants].astype(BF)
    sums_ref[:, :, quarter:] = jnp.zeros((sums_ref.shape[0], tenants, PAD), BF)
    for index in range(packs_ref.shape[0]):
        sums_ref[partner_of(index, sums_ref.shape[0] // 2), :, quarter:] = packs_ref[index]


def finish_kernel(got_ref, grad_ref, low_ref):
    holders, rows_out, padded = got_ref.shape
    width = padded - PAD
    total = got_ref[0, :, :width].astype(F32)
    for holder in range(1, holders):
        total = total + got_ref[holder, :, :width].astype(F32)
    grad_ref[...] = total
    rank, tokens = low_ref.shape
    sharers, held = len(STEPS), len(STEPS[0])
    blocks = sharers * held
    block_size = tokens // blocks
    packs = [
        got_ref[partner_of(index, holders // 2), :, width:].astype(F32) for index in range(sharers)
    ]
    span = held * block_size
    columns = jnp.concatenate(
        [
            jnp.concatenate([pack[:, group * span : (group + 1) * span] for pack in packs], axis=1)
            for group in range(rank // rows_out)
        ],
        axis=0,
    ).astype(BF)
    row = lax.broadcasted_iota(jnp.int32, (block_size, tokens), 0)
    lane = lax.broadcasted_iota(jnp.int32, (block_size, tokens), 1)
    kind, place = own_kind(), lax.axis_index("z")
    starts = [
        (step_of(kind ^ index, turn) + place) % blocks * block_size
        for index in range(sharers)
        for turn in range(held)
    ]
    moves = jnp.concatenate(
        [jnp.where(lane == start + row, 1.0, 0.0) for start in starts], axis=0
    ).astype(BF)
    low_ref[...] = jnp.dot(columns, moves, preferred_element_type=F32).astype(BF)


def per_device(
    d_out, normed, rstd, gain, expert_grads, expert_ids, low_rank, lengths, tenant_ids, adapters
):
    tok_count, model_width = d_out.shape
    expert_count, slot_count = expert_grads.shape[2], expert_grads.shape[3]
    tenant_count = lax.axis_size("z")
    block_size = tok_count // tenant_count
    ten_dev, rank_size = adapters.shape[0], adapters.shape[1]
    y_count = lax.axis_size("y")

    returned = exchange(expert_grads[0, 0], ("y", "x", "c"))

    x_count, c_count = lax.axis_size("x"), lax.axis_size("c")
    sharers, held = len(STEPS), len(STEPS[0])
    shard = adapters.reshape(ten_dev * rank_size, model_width)
    shards = [
        lax.ppermute(
            shard,
            ("z", "x", "c"),
            [
                (
                    ((z + STEPS[x % 2 * 2 + c][turn]) % tenant_count * x_count + x) * c_count + c,
                    (z * x_count + x) * c_count + c,
                )
                for z in range(tenant_count)
                for x in range(x_count)
                for c in range(c_count)
            ],
        )
        for turn in range(held)
    ]
    shards = [pltpu.with_memory_space_constraint(array, pltpu.HBM) for array in shards]
    local_ids = tenant_ids - jnp.arange(tenant_count, dtype=jnp.int32) * ten_dev
    routes = expert_ids[:, 0]
    onehot = (routes[:, None] == jnp.arange(expert_count, dtype=jnp.int32)[None, :]).astype(F32)
    position = jnp.arange(tok_count, dtype=jnp.int32)
    earlier = (position[:, None] > position[None, :]).astype(F32)
    before = jnp.dot(earlier, onehot, preferred_element_type=F32)
    slot_ids = jnp.sum(before * onehot, axis=1).astype(jnp.int32)
    flat_slot = routes * slot_count + slot_ids
    pick = (
        flat_slot[:, None] == jnp.arange(expert_count * slot_count, dtype=jnp.int32)[None, :]
    ).astype(BF)
    valid = (
        jnp.arange(block_size, dtype=jnp.int32)[None, :] < lengths[:, None]
    ).reshape(tok_count, 1)
    zero = jnp.zeros((), BF)
    rstd_kept = jnp.where(valid, rstd[:, None], 0.0)
    normed_kept = jnp.where(valid, normed, zero)
    block_of = position // block_size
    low_t = jnp.broadcast_to(
        low_rank.T.reshape(y_count, 1, 2, tok_count), (y_count, tenant_count, 2, tok_count)
    ).reshape(tok_count, tok_count)
    row_block = position // 2 % tenant_count
    spread = jnp.where(row_block[:, None] == block_of[None, :], low_t, zero)
    marks = jnp.broadcast_to(local_ids.astype(BF)[None, :, None, None], (y_count, tenant_count, 2, PAD))
    spread = jnp.concatenate([spread, marks.reshape(tok_count, PAD)], axis=1)

    vmem = pl.BlockSpec(memory_space=pltpu.VMEM)
    grant = pltpu.CompilerParams(vmem_limit_bytes=24 * 1024 * 1024)
    hbm = pl.BlockSpec(memory_space=pl.ANY)
    terms_shape = (tenant_count * y_count, 2, model_width + PAD)
    terms, *cots = pl.pallas_call(
        cotangent_kernel,
        out_shape=(
            pltpu.HBM(terms_shape, BF),
            *[pltpu.HBM((held, block_size, model_width + PAD), BF)] * sharers,
        ),
        in_specs=[vmem] * 6 + [hbm] * (1 + held),
        out_specs=(hbm,) * (1 + sharers),
        scratch_shapes=[pltpu.VMEM((tok_count, model_width), BF)] * 2
        + [
            pltpu.VMEM((tok_count, model_width + PAD), BF),
            pltpu.VMEM(terms_shape, BF),
            pltpu.SemaphoreType.DMA((PIECES,)),
            pltpu.SemaphoreType.DMA((tenant_count + model_width // CHUNK,)),
        ],
        compiler_params=grant,
        name="cotangent",
    )(
        returned,
        pick,
        gain[None, :],
        rstd_kept,
        spread,
        normed_kept,
        pltpu.with_memory_space_constraint(d_out, pltpu.HBM),
        *shards,
    )

    arrived = exchange(terms, ("y", "z"))

    def swap(array, turn):
        pairs = [
            (x * c_count + c, (x ^ (turn >> 1)) * c_count + (c ^ (turn & 1)))
            for x in range(x_count)
            for c in range(c_count)
        ]
        return lax.ppermute(array, ("x", "c"), pairs)

    came = [cots[0]] + [swap(cots[turn], turn) for turn in range(1, sharers)]
    column_parts = x_count * c_count
    packs = pl.pallas_call(
        low_rank_kernel,
        out_shape=jax.ShapeDtypeStruct((sharers, ten_dev, PAD), BF),
        in_specs=[vmem] * sharers + [hbm] * held,
        out_specs=vmem,
        scratch_shapes=[pltpu.VMEM(shard.shape, BF)] * held + [pltpu.SemaphoreType.DMA((held,))],
        compiler_params=grant,
        cost_estimate=pl.CostEstimate(flops=1 << 20, bytes_accessed=1 << 20, transcendentals=0),
        name="low_rank",
    )(*came, *shards)
    sums = pl.pallas_call(
        sum_kernel,
        out_shape=jax.ShapeDtypeStruct(
            (column_parts, ten_dev, 2 * model_width // column_parts + PAD), BF
        ),
        in_specs=[vmem, vmem],
        out_specs=vmem,
        compiler_params=grant,
        name="tenant_sums",
    )(arrived, packs)
    grad_b, low_columns = pl.pallas_call(
        finish_kernel,
        out_shape=(
            jax.ShapeDtypeStruct((ten_dev, 2 * model_width // column_parts), F32),
            jax.ShapeDtypeStruct((rank_size, tok_count), BF),
        ),
        in_specs=[vmem],
        out_specs=(vmem, vmem),
        compiler_params=grant,
        name="finish",
    )(exchange(sums, ("c", "x")))
    return (grad_b, low_columns.T)


def solution(mesh):
    fine = Mesh(mesh.devices.reshape(8, 8, 4, 2), ALL)
    expert = ("y", "x", "c")
    placed = (
        P(ALL, None),
        P(ALL, None),
        P(ALL),
        P(),
        P("z", expert, None, None, None),
        P(ALL, None),
        P(ALL, None),
        P(ALL),
        P(ALL),
        P("z", None, None),
    )
    return jax.shard_map(
        per_device,
        mesh=fine,
        in_specs=placed,
        out_specs=(P("z", expert), P(ALL, None)),
        check_vma=False,
    )
```
